128 devices in a mesh: dp: 32 (over z, y, core), segment: 2 (over x_hi), frame: 2 (over x_lo).
Axes of the slice: x: 4 (x_hi: 2, x_lo: 2; x = x_hi * 2 + x_lo), y: 4, z: 4, core: 2. Of those that a mesh axis runs over, the one named last changes fastest.
Arguments:
- frames_in: bfloat16 [32, 256, 4096], P('dp', 'frame'), may hold values from -6 to 6
- qkv_weight: bfloat16 [2, 4096, 3, 2048], P('segment', 'dp', None, 'frame'), may hold values from -3 to 3
- out_weight: bfloat16 [2, 2048, 4096], P('segment', 'frame', 'dp'), may hold values from -0.125 to 0.125
- proj_weight: bfloat16 [4096, 1024], replicated, may hold values from -0.09375 to 0.09375
- depth_qkv: bfloat16 [1024, 3, 512], replicated, may hold values from -5 to 5
- depth_out: bfloat16 [512, 1024], replicated, may hold values from -0.25 to 0.25
- code_table: bfloat16 [2048, 1024], replicated, may hold values from -6 to 6
- logit_weight: bfloat16 [1024, 2048], replicated, may hold values from -24 to 24
- codes: int32 [32, 256, 6], P('dp', 'frame'), may hold values from 0 to 2047
- delays: int32 [6], replicated, may hold values from 0 to 2
Outputs:
- losses: float32 [32, 256, 6], P('dp', 'frame')
The draws below stay inside these ranges and needn't reach their ends.
All inputs are finite; a program needn't handle non-finite values.
Results may differ from the reference program's by a relative error of at most 0.005.
Values may be sent and summed in bfloat16 or wider, within the bound.
No kernel may reach another device: no remote copies, remote signals or barrier semaphores. Data moves between devices by JAX's collectives and lax.ppermute only.
A program may use at most 192 MiB of HBM per device.

```python
import math
import jax
import jax.numpy as jnp
from jax import lax

D = 4096
HT = 16
HD = 128
DD = 1024
HDEP = 8
HDD = 64
CARD = 2048
K = 6
DMAX = 2
FRAMES = 256
SEGMENTS = 2
DIALOGS = 32


def codebook_entries(key):
    return jax.random.truncated_normal(key, -6.0, 6.0, (CARD, DD), jnp.float32)


def draw_qkv_weight(key, part):
    key = jax.random.fold_in(key, 11)
    base_key = jax.random.fold_in(key, 0)
    base_values = jax.random.truncated_normal(base_key, -4.0, 4.0, (SEGMENTS, D, 3, HT, HD), jnp.float32) / math.sqrt(D)
    return base_values.reshape(SEGMENTS, D, 3, HT * HD).astype(jnp.bfloat16)


def draw_depth_qkv(key, part):
    key = jax.random.fold_in(key, 12)
    base_key = jax.random.fold_in(key, 0)
    base_values = jax.random.truncated_normal(base_key, -4.0, 4.0, (DD, 3, HDEP, HDD), jnp.float32) / math.sqrt(DD)
    return base_values.reshape(DD, 3, HDEP * HDD).astype(jnp.bfloat16)


def draw_code_table(key, part):
    code_values = codebook_entries(key)
    return code_values.astype(jnp.bfloat16)


def draw_logit_weight(key, part):
    key = jax.random.fold_in(key, 17)
    base_key, scale_key = jax.random.split(key, 2)
    scales = jnp.exp(jax.random.uniform(scale_key, (1, CARD), jnp.float32, math.log(1.5), math.log(6.0)))
    weight = jax.random.truncated_normal(base_key, -4.0, 4.0, (DD, CARD), jnp.float32) * scales / math.sqrt(DD)
    return weight.astype(jnp.bfloat16)


def set_ends(values, key, smallest, largest):
    index_at = [jax.random.randint(jax.random.fold_in(key, axis), (), 0, length) for axis, length in enumerate(values.shape)]
    widest = values.shape.index(max(values.shape))
    next_to = index_at[:widest] + [(index_at[widest] + 1) % values.shape[widest]] + index_at[widest + 1:]
    return values.at[tuple(index_at)].set(smallest).at[tuple(next_to)].set(largest)


def levels(rng, dims, shards, low, top_value):
    gain, own = 1.0, jax.random.fold_in(rng, 6)
    for position, shards_of in shards:
        draws = jnp.exp(jax.random.uniform(jax.random.fold_in(own, position), (shards_of,), jnp.float32, low / len(shards), top_value / len(shards)))
        gain = gain * jnp.repeat(draws, dims[position] // shards_of).reshape([-1 if axis == position else 1 for axis in range(len(dims))])
    return gain


def normal_values(key, shape, deviation, limit, cuts=(), kind=jnp.bfloat16):
    entries = jax.random.normal(key, shape, jnp.float32) * deviation
    if len(cuts) > 0:
        entries = levels(key, shape, cuts, -0.22, 0.18) * entries
    return jnp.clip(entries, min=-limit, max=limit).astype(kind)


def setup_inputs(seed: int = 0) -> dict:
    arg_keys = jax.random.split(jax.random.key(seed), 11)
    return {
        "frames_in": normal_values(arg_keys[0], (DIALOGS, FRAMES, D), 1.0, 6.0, ((0, 32), (1, 2))),
        "qkv_weight": draw_qkv_weight(jax.random.fold_in(arg_keys[10], 71), 0),
        "out_weight": normal_values(arg_keys[2], (SEGMENTS, HT * HD, D), (HT * HD) ** -0.5, 0.125, ((0, 2), (1, 2), (2, 32))),
        "proj_weight": normal_values(arg_keys[3], (D, DD), D ** -0.5, 0.09375),
        "depth_qkv": draw_depth_qkv(jax.random.fold_in(arg_keys[10], 71), 0),
        "depth_out": normal_values(arg_keys[5], (HDEP * HDD, DD), (HDEP * HDD) ** -0.5, 0.25),
        "code_table": draw_code_table(jax.random.fold_in(arg_keys[10], 71), 0),
        "logit_weight": draw_logit_weight(jax.random.fold_in(arg_keys[10], 71), 0),
        "codes": set_ends(jax.random.randint(arg_keys[8], (DIALOGS, FRAMES, K), 0, CARD), jax.random.fold_in(arg_keys[8], 1), 0, CARD - 1).astype(jnp.int32),
        "delays": set_ends(jax.random.randint(arg_keys[9], (K,), 0, DMAX + 1), jax.random.fold_in(arg_keys[9], 1), 0, DMAX).astype(jnp.int32),
    }


def rms_round(values):
    scale = lax.rsqrt(lax.optimization_barrier(jnp.mean(values * values, axis=-1, keepdims=True)) + 1e-05)
    return (values * scale).astype(jnp.bfloat16)

def rotate(values, positions):
    half_width = values.shape[-1] // 2
    frequency = 10000.0 ** (-jnp.arange(half_width, dtype=jnp.float32) / half_width)
    angles = positions[:, None].astype(jnp.float32) * frequency[None, :]
    cosine = jnp.cos(angles)[:, None, :]
    sine = jnp.sin(angles)[:, None, :]
    first = values[..., :half_width]
    second = values[..., half_width:]
    return jnp.concatenate([first * cosine - second * sine, first * sine + second * cosine], axis=-1)

def attend(projected, head_size, positions):
    row_count = projected.shape[0]
    split = projected.reshape(row_count, 3, -1, head_size)
    queries = rotate(split[:, 0], positions).astype(jnp.bfloat16).astype(jnp.float32)
    keys = rotate(split[:, 1], positions).astype(jnp.bfloat16).astype(jnp.float32)
    values = split[:, 2].astype(jnp.bfloat16).astype(jnp.float32)
    scores = jnp.einsum('qhd,khd->hqk', queries, keys) / jnp.sqrt(jnp.float32(head_size))
    causal_mask = positions[:, None] >= positions[None, :]
    scores = jnp.where(causal_mask[None], scores, -1e+30)
    weights = jax.nn.softmax(scores, axis=-1).astype(jnp.bfloat16).astype(jnp.float32)
    context = jnp.einsum('hqk,khd->qhd', weights, values)
    return context.reshape(row_count, -1).astype(jnp.bfloat16)

def depth_loss(depth_in, targets, is_valid, depth_qkv, depth_out, code_table, logit_weight):
    count, streams = targets.shape
    width = depth_in.shape[1]
    safe = jnp.clip(targets, 0, code_table.shape[0] - 1).astype(jnp.int32)
    embedded = jnp.take(code_table, safe[:, :-1], axis=0).astype(jnp.float32)
    embedded = embedded * is_valid[:, :-1, None].astype(jnp.float32)
    embedded = jnp.concatenate([jnp.zeros((count, 1, width), jnp.float32), embedded], axis=1)
    inputs = depth_in.astype(jnp.float32)[:, None, :] + embedded
    normed = rms_round(inputs).reshape(count * streams, width)
    head_width = depth_out.shape[0]
    projected = jnp.dot(normed, depth_qkv.reshape(width, 3 * head_width), preferred_element_type=jnp.float32)
    split = projected.reshape(count, streams, 3, -1, HDD).astype(jnp.bfloat16).astype(jnp.float32)
    scores = jnp.einsum('fqhd,fkhd->fhqk', split[:, :, 0], split[:, :, 1]) / jnp.sqrt(jnp.float32(HDD))
    order = jnp.arange(streams)
    scores = jnp.where((order[:, None] >= order[None, :])[None, None], scores, -1e+30)
    weights = jax.nn.softmax(scores, axis=-1).astype(jnp.bfloat16).astype(jnp.float32)
    context = jnp.einsum('fhqk,fkhd->fqhd', weights, split[:, :, 2]).reshape(count * streams, head_width).astype(jnp.bfloat16)
    mixed_rows = inputs.reshape(count * streams, width) + jnp.dot(context, depth_out, preferred_element_type=jnp.float32)
    logits = jnp.dot(rms_round(mixed_rows), logit_weight, preferred_element_type=jnp.float32)
    log_total = jax.nn.logsumexp(logits, axis=-1)
    picked = jnp.take_along_axis(logits, safe.reshape(-1, 1), axis=1)[:, 0]
    return jnp.where(is_valid, (log_total - picked).reshape(count, streams), 0.0)

def temporal_layer(inputs, qkv_layer, out_layer):
    positions = jnp.arange(inputs.shape[0])
    normed = rms_round(inputs.astype(jnp.float32))
    projected = jnp.dot(normed, qkv_layer.reshape(qkv_layer.shape[0], -1), preferred_element_type=jnp.float32)
    context = attend(projected, HD, positions)
    mixed_out = jnp.dot(context, out_layer, preferred_element_type=jnp.float32)
    return (inputs.astype(jnp.float32) + mixed_out).astype(jnp.bfloat16)

def reference(frames_in, qkv_weight, out_weight, proj_weight, depth_qkv, depth_out, code_table, logit_weight, codes, delays):

    def one_dialog(members):
        hidden, dialog_codes = members
        for section in range(SEGMENTS):
            hidden = temporal_layer(hidden, qkv_weight[section], out_weight[section])
        depth_in = jnp.dot(rms_round(hidden.astype(jnp.float32)), proj_weight, preferred_element_type=jnp.float32).astype(jnp.bfloat16)
        source = (jnp.arange(FRAMES, dtype=jnp.int32)[:, None] - delays[None, :]).astype(jnp.int32)
        is_valid = source >= 0
        targets = jnp.take_along_axis(dialog_codes, jnp.maximum(source, 0).astype(jnp.int32), axis=0)
        return depth_loss(depth_in, targets, is_valid, depth_qkv, depth_out, code_table, logit_weight)
    return lax.map(one_dialog, (frames_in, codes))
```

```python
import functools

import jax
import jax.numpy as jnp
from jax import lax
from jax.experimental import pallas as pl
from jax.experimental.pallas import tpu as pltpu
from jax.sharding import PartitionSpec as P

HD = 128
DMAX = 2
ZN, YN = 4, 4
SIDE = 4
BF = jnp.bfloat16
F32 = jnp.float32
EPS = 1e-05


def hop(value, axis, sign=1):
    pairs = []
    for z in range(ZN):
        for y in range(YN):
            for c in range(2):
                step = sign * (1 - 2 * c)
                there = {
                    "z": ((z + step) % ZN, y, c),
                    "y": (z, (y + step) % YN, c),
                    "core": (z, y, 1 - c),
                }[axis]
                pairs.append(
                    ((z * YN + y) * 2 + c, (there[0] * YN + there[1]) * 2 + there[2])
                )
    return lax.ppermute(value, "dp", pairs)


def xswap(value, pairs):
    return lax.ppermute(value, ("segment", "frame"), pairs)


def xhop(value, sign):
    pairs = []
    for d in range(2 * ZN * YN):
        step = sign * (1 - 2 * (d % 2))
        pairs += [(d * SIDE + i, d * SIDE + (i + step) % SIDE) for i in range(SIDE)]
    return lax.ppermute(value, ("dp", "segment", "frame"), pairs)


def tied(values, after):
    return lax.optimization_barrier((values, after))[0]


ORDER = (0, 1, -1, 2)


def ring(first, second):
    each = (first, second)
    near = [[hop(block, axis), hop(block, axis, -1)] for axis, block in each]
    near, blocks = lax.optimization_barrier((near, [first[1], second[1]]))
    far = [hop(ahead, axis) for (axis, _), (ahead, _) in zip(each, near)]
    return [[block, *two, one] for block, two, one in zip(blocks, near, far)]


def gather(a, b):
    a, b = ring(("z", a), ("y", b))
    a, b = jnp.concatenate(a), jnp.concatenate(b)
    a, b = ring(("y", a), ("z", b))
    return [p for mine in (a, b) for p in mine + [hop(block, "core") for block in mine]]


def vmem():
    return pl.BlockSpec(memory_space=pltpu.VMEM)


def smem():
    return pl.BlockSpec(memory_space=pltpu.SMEM)


def anywhere():
    return pl.BlockSpec(memory_space=pl.ANY)


def rms(values):
    scale = lax.rsqrt(jnp.mean(values * values, axis=-1, keepdims=True) + EPS)
    return (values * scale).astype(BF)


def norm_kernel(x_ref, o_ref):
    o_ref[...] = rms(x_ref[...].astype(F32))


def norm_rows(x):
    return pl.pallas_call(
        norm_kernel,
        out_shape=jax.ShapeDtypeStruct(x.shape, BF),
        in_specs=[vmem()],
        out_specs=vmem(),
        name="norm_rows",
    )(x)


def summed(*refs):
    total = refs[0][...].astype(F32)
    for ref in refs[1:]:
        total = total + ref[...].astype(F32)
    return total.astype(BF)


def merge_kernel(x_ref, a_ref, b_ref, c_ref, x_out, n_out):
    new = summed(x_ref, a_ref, b_ref, c_ref)
    x_out[...] = new
    n_out[...] = rms(new.astype(F32))


def merge_rows(x, parts):
    return pl.pallas_call(
        merge_kernel,
        out_shape=[jax.ShapeDtypeStruct(x.shape, BF)] * 2,
        in_specs=[vmem()] * 4,
        out_specs=[vmem()] * 2,
        name="merge_rows",
    )(x, *parts)


def softmax_rounded(scores):
    top = jnp.max(scores, axis=-1, keepdims=True)
    weights = jnp.exp(scores - top)
    return (weights / jnp.sum(weights, axis=-1, keepdims=True)).astype(BF)


NT = (((1,), (1,)), ((), ()))


def layer_kernel(x_count, w_count, *refs):
    place, cos_ref, sin_ref = refs[:3]
    at = 3 + x_count
    x_refs, w_refs = refs[3:at], refs[at : at + w_count]
    outs = refs[at + w_count : at + w_count + SIDE]
    x_s, w_s, ctx_s, out_s, x_sem, w_sem, o_sem = refs[at + w_count + SIDE :]
    z, y, c = place[0], place[1], place[2]

    def chunk_of(piece, j):
        near, far = (j, piece % 4) if piece < 8 else (piece % 4, j)
        core = c if piece % 8 < 4 else 1 - c
        step = 2 * core - 1
        far_z, far_y = z + step * ORDER[near], y + step * ORDER[far]
        return ((far_z & 3) * YN + (far_y & 3)) * 2 + core

    for i, ref in enumerate(x_refs):
        start = pl.multiple_of(place[3 + i], 64)
        pltpu.make_async_copy(ref, x_s.at[pl.ds(start, ref.shape[0])], x_sem).start()
    for half in range(2):
        if w_count == 1:
            pltpu.make_async_copy(
                w_refs[0].at[:, half], w_s.at[half], w_sem.at[half]
            ).start()
            continue
        for i in range(8 * half, 8 * half + 8):
            for j in range(4):
                pltpu.make_async_copy(
                    w_refs[i].at[pl.ds(128 * j, 128)],
                    w_s.at[half, chunk_of(i, j)],
                    w_sem.at[half],
                ).start()

    pltpu.make_async_copy(x_s, x_s, x_sem).wait()
    rows = x_s.shape[0]
    lower = lax.broadcasted_iota(jnp.int32, (rows, rows), 0) >= lax.broadcasted_iota(
        jnp.int32, (rows, rows), 1
    )
    cosine, sine = cos_ref[...], sin_ref[...]
    scale = 1.0 / jnp.sqrt(F32(HD))

    def turned(v):
        return (v * cosine + pltpu.roll(v, HD // 2, 1) * sine).astype(BF)

    width = x_s.shape[1]
    for half in range(2):
        pltpu.make_async_copy(w_s.at[half], w_s.at[half], w_sem.at[half]).wait()
        q, k, v = (
            jnp.dot(
                x_s[...],
                w_s[half, :, :, 256 * i : 256 * i + 256].reshape(width, 256),
                preferred_element_type=F32,
            )
            for i in range(3)
        )
        for head in range(2):
            cut = slice(head * HD, head * HD + HD)
            scores = lax.dot_general(
                turned(q[:, cut]), turned(k[:, cut]), NT, preferred_element_type=F32
            )
            weights = softmax_rounded(jnp.where(lower, scores * scale, -1e30))
            context = jnp.dot(weights, v[:, cut].astype(BF), preferred_element_type=F32)
            ctx_s[half, :, cut] = context.astype(BF)

    tile = 512

    def project(n, _):
        total = None
        for half in range(2):
            part = lax.dot_general(
                ctx_s[half],
                w_s[half, pl.ds(n * (tile // 128), tile // 128), :, 768:].reshape(tile, 256),
                NT, preferred_element_type=F32,
            )
            total = part if total is None else total + part
        out_s[:, pl.ds(pl.multiple_of(n * tile, tile), tile)] = total.astype(BF)
        return _

    lax.fori_loop(0, out_s.shape[1] // tile, project, 0)
    copies = []
    for i, ref in enumerate(outs):
        start = pl.multiple_of(place[8 + i], 64)
        copies.append(
            pltpu.make_async_copy(out_s.at[pl.ds(start, 64)], ref, o_sem.at[i])
        )
        copies[-1].start()
    for copy in copies:
        copy.wait()


def layer(place, cosine, sine, x_blocks, weights):
    width = x_blocks[0].shape[1]
    rows = sum(b.shape[0] for b in x_blocks)
    return pl.pallas_call(
        functools.partial(layer_kernel, len(x_blocks), len(weights)),
        out_shape=[jax.ShapeDtypeStruct((64, width), BF)] * SIDE,
        in_specs=[smem(), vmem(), vmem()]
        + [anywhere()] * (len(x_blocks) + len(weights)),
        out_specs=[anywhere()] * SIDE,
        scratch_shapes=[
            pltpu.VMEM((rows, width), BF),
            pltpu.VMEM((2, width // 128, 128, 1024), BF),
            pltpu.VMEM((2, rows, 256), BF),
            pltpu.VMEM((rows, width), BF),
            pltpu.SemaphoreType.DMA,
            pltpu.SemaphoreType.DMA((2,)),
            pltpu.SemaphoreType.DMA((SIDE,)),
        ],
        compiler_params=pltpu.CompilerParams(vmem_limit_bytes=56 * 2**20),
        cost_estimate=pl.CostEstimate(
            flops=2 * rows * width * 2048, bytes_accessed=2**24, transcendentals=0
        ),
        name="layer",
    )(place, cosine, sine, *x_blocks, *weights)


TF = 16


def depth_kernel(x_ref, a_ref, b_ref, c_ref, proj, dqkv, dout, logit, emb, target,
                 o_ref, u_s, qkv_s, ctx_s):
    new = summed(x_ref, a_ref, b_ref, c_ref)
    normed = rms(new.astype(F32))
    depth_in = jnp.dot(normed, proj[...], preferred_element_type=F32).astype(BF)
    depth_in = depth_in.astype(F32)
    frames = x_ref.shape[0]
    streams = u_s.shape[0] // frames
    span = TF * streams
    for tile in range(frames // TF):
        base = depth_in[tile * TF : tile * TF + TF]
        for k in range(streams):
            cut = slice(tile * span + k * TF, tile * span + k * TF + TF)
            u_s[cut] = base + emb[cut].astype(F32)
    inputs = rms(u_s[...])
    for i in range(3):
        qkv_s[i] = jnp.dot(inputs, dqkv[i], preferred_element_type=F32).astype(BF)
    r = lax.broadcasted_iota(jnp.int32, (span, span), 0)
    q = lax.broadcasted_iota(jnp.int32, (span, span), 1)
    seen = ((r & (TF - 1)) == (q & (TF - 1))) & (r >= q)
    head_width = dout.shape[0]
    lane = lax.broadcasted_iota(jnp.int32, (span, 128), 1)
    for tile in range(frames // TF):
        rows = slice(tile * span, tile * span + span)
        for pair in range(head_width // 128):
            cut = slice(pair * 128, pair * 128 + 128)
            queries, keys, values = (qkv_s[i, rows, cut] for i in range(3))
            both = []
            for head in range(2):
                mine = (lane < 64) if head == 0 else (lane >= 64)
                scores = lax.dot_general(
                    jnp.where(mine, queries, jnp.zeros_like(queries)),
                    keys, NT, preferred_element_type=F32,
                )
                weights = softmax_rounded(jnp.where(seen, scores * 0.125, -1e30))
                both.append(jnp.dot(weights, values, preferred_element_type=F32))
            ctx_s[rows, cut] = jnp.where(lane < 64, both[0], both[1]).astype(BF)
    mixed = u_s[...] + jnp.dot(ctx_s[...], dout[...], preferred_element_type=F32)
    logits = jnp.dot(rms(mixed), logit[...], preferred_element_type=F32)
    top = jnp.max(logits, axis=-1, keepdims=True)
    total = jnp.sum(jnp.exp(logits - top), axis=-1, keepdims=True)
    entry = lax.broadcasted_iota(jnp.int32, logits.shape, 1)
    picked = jnp.sum(jnp.where(entry == target[...], logits, 0.0), axis=-1, keepdims=True)
    o_ref[...] = jnp.log(total) + top - picked


def depth(x, parts, proj, dqkv, dout, logit, emb, target):
    count, width = emb.shape
    head_width = dout.shape[0]
    return pl.pallas_call(
        depth_kernel,
        out_shape=jax.ShapeDtypeStruct((count, 1), F32),
        in_specs=[vmem()] * 10,
        out_specs=vmem(),
        scratch_shapes=[
            pltpu.VMEM((count, width), F32),
            pltpu.VMEM((3, count, head_width), BF),
            pltpu.VMEM((count, head_width), BF),
        ],
        compiler_params=pltpu.CompilerParams(vmem_limit_bytes=48 * 2**20),
        cost_estimate=pl.CostEstimate(
            flops=2 * count * width * 5120, bytes_accessed=2**24, transcendentals=0
        ),
        name="depth",
    )(x, *parts, proj, dqkv, dout, logit, emb, target)


def rope_tables(rows):
    half = HD // 2
    frequency = 10000.0 ** (-jnp.arange(half, dtype=F32) / half)
    angles = jnp.arange(rows).astype(F32)[:, None] * frequency[None, :]
    cosine, sine = jnp.cos(angles), jnp.sin(angles)
    return (
        jnp.concatenate([cosine, cosine], axis=1),
        jnp.concatenate([-sine, sine], axis=1),
    )


def packed_weights(qkv_weight, out_weight):
    w = jnp.transpose(qkv_weight[0], (1, 0, 2))
    o = out_weight[0]
    blocks = []
    for i in range(4):
        cut = slice(256 * i, 256 * i + 256)
        blocks.append(
            jnp.concatenate([w[0][:, cut], w[1][:, cut], w[2][:, cut], o[cut].T], axis=1)
        )
    return jnp.stack(blocks).reshape(2, 2, 128, 1024)


def local(
    frames_in, qkv_weight, out_weight, proj_weight, depth_qkv, depth_out, code_table,
    logit_weight, codes, delays,
):
    s = lax.axis_index("segment")
    f = lax.axis_index("frame")
    d = lax.axis_index("dp")
    z, y, c = d // (YN * 2), (d // 2) % YN, d % 2
    row_count = frames_in.shape[1]
    part = row_count // 2
    streams = codes.shape[2]
    me = s * 2 + f

    def rows_of(i):
        i = i % SIDE
        return (i % 2) * row_count + (i // 2) * part

    sign = 1 - 2 * c

    def place_of(starts):
        starts = (list(starts) + [0] * 5)[:5]
        targets = [rows_of(me + k * sign + 4) for k in (0, 1, 2, 3)]
        return jnp.stack([z, y, c, *starts, *targets]).astype(jnp.int32)

    packed = packed_weights(qkv_weight, out_weight)
    kept = lax.dynamic_index_in_dim(packed, s, 0, keepdims=False)
    given = lax.dynamic_index_in_dim(packed, 1 - s, 0, keepdims=False)
    got = xswap(given, [(0, 3), (3, 0), (1, 2), (2, 1)])
    first = jnp.where(s == 0, kept, got)
    second = jnp.where(s == 0, got, kept)
    frames = frames_in[0]
    normed = norm_rows(frames)
    far = xhop(tied(normed, got), 1)

    w0 = gather(first[0], first[1])
    w1 = [lax.all_gather(tied(second, (w0[1], w0[2], w0[9], w0[10])), "dp")]

    tail = lax.ppermute(codes[0, row_count - DMAX :], "frame", [(0, 1)])
    extended = jnp.concatenate([tail, codes[0]], axis=0)
    extended = lax.dynamic_slice_in_dim(extended, s * part, part + DMAX, 0)
    targets = extended[DMAX : DMAX + part]
    for lag in range(1, DMAX + 1):
        targets = jnp.where(
            delays[None, :] == lag, extended[DMAX - lag : DMAX - lag + part], targets
        )
    frame = rows_of(me) + jnp.arange(part, dtype=jnp.int32)
    is_valid = frame[:, None] >= delays[None, :]
    targets = jnp.clip(targets, 0, code_table.shape[0] - 1)

    def tiled(a):
        return jnp.transpose(a.reshape(part // TF, TF, streams), (0, 2, 1)).reshape(-1)

    def behind(a):
        return jnp.concatenate([jnp.zeros_like(a[:, :1]), a[:, :-1]], axis=1)

    emb = jnp.take(code_table, tiled(behind(targets)), axis=0, mode="clip")
    emb = jnp.where(tiled(behind(is_valid))[:, None], emb, jnp.zeros_like(emb))

    cosine, sine = tied(rope_tables(2 * row_count), emb)
    sent = layer(
        place_of([f * row_count, (1 - f) * row_count]), cosine, sine, [normed, far], w0
    )

    def scattered(sent):
        back = xhop(sent[3], -1)
        relayed = xhop(sent[2], 1)
        relayed = (sent[1].astype(F32) + relayed.astype(F32)).astype(BF)
        return [sent[0], xhop(relayed, 1), back]

    mine = lax.dynamic_slice_in_dim(frames, s * part, part, 0)
    x1, n1 = merge_rows(mine, scattered(sent))
    ahead = xhop(n1, 1)
    blocks = [n1, ahead, xhop(n1, -1), xhop(ahead, 1)]
    starts = [rows_of(me + k * sign + 4) for k in (0, -1, 1, -2)]
    sent = layer(place_of(starts), cosine, sine, blocks, w1)

    losses = depth(
        x1, scattered(sent), proj_weight, jnp.transpose(depth_qkv, (1, 0, 2)),
        depth_out, logit_weight, emb, tiled(targets)[:, None],
    )
    losses = jnp.transpose(losses.reshape(part // TF, streams, TF), (0, 2, 1))
    losses = jnp.where(is_valid, losses.reshape(part, streams), 0.0)
    other = xswap(losses, [(i, (i + 2) % SIDE) for i in range(SIDE)])
    both = jnp.where(s == 0, jnp.stack([losses, other]), jnp.stack([other, losses]))
    return both.reshape(1, row_count, streams)


def solution(mesh):
    return jax.shard_map(
        local,
        mesh=mesh,
        in_specs=(
            P("dp", "frame", None),
            P("segment", "dp", None, "frame"),
            P("segment", "frame", "dp"),
            P(),
            P(),
            P(),
            P(),
            P(),
            P("dp", "frame", None),
            P(),
        ),
        out_specs=P("dp", "frame", None),
        check_vma=False,
    )
```

```python
import functools

import jax
import jax.numpy as jnp
from jax import lax
from jax.experimental import pallas as pl
from jax.experimental.pallas import tpu as pltpu
from jax.sharding import PartitionSpec as P

HD = 128
HDD = 64
DMAX = 2
ZN, YN = 4, 4
SIDE = 4
BF = jnp.bfloat16
F32 = jnp.float32
EPS = 1e-05


def xswap(value, pairs):
    return lax.ppermute(value, ("segment", "frame"), pairs)


def xhop(value, sign):
    pairs = []
    for d in range(2 * ZN * YN):
        step = sign * (1 - 2 * (d % 2))
        pairs += [(d * SIDE + i, d * SIDE + (i + step) % SIDE) for i in range(SIDE)]
    return lax.ppermute(value, ("dp", "segment", "frame"), pairs)


def tied(values, after):
    return lax.optimization_barrier((values, after))[0]


def xhop2(value):
    return xswap(value, [(i, (i + 2) % SIDE) for i in range(SIDE)])


def vmem():
    return pl.BlockSpec(memory_space=pltpu.VMEM)


def smem():
    return pl.BlockSpec(memory_space=pltpu.SMEM)


def anywhere():
    return pl.BlockSpec(memory_space=pl.ANY)


def rms(values):
    scale = lax.rsqrt(jnp.mean(values * values, axis=-1, keepdims=True) + EPS)
    return (values * scale).astype(BF)


def norm_kernel(x_ref, o_ref):
    o_ref[...] = rms(x_ref[...].astype(F32))


def norm_rows(x):
    return pl.pallas_call(
        norm_kernel,
        out_shape=pltpu.HBM(x.shape, BF),
        in_specs=[vmem()],
        out_specs=vmem(),
        compiler_params=pltpu.CompilerParams(vmem_limit_bytes=8 * 2**20),
        name="norm_rows",
    )(x)


def summed(*refs):
    total = refs[0][...].astype(F32)
    for ref in refs[1:]:
        total = total + ref[...].astype(F32)
    return total.astype(BF)


def merge_kernel(x_ref, a_ref, b_ref, c_ref, d_ref, x_out, n_out):
    new = summed(x_ref, a_ref, b_ref, c_ref, d_ref)
    x_out[...] = new
    n_out[...] = rms(new.astype(F32))


def merge_rows(x, parts):
    return pl.pallas_call(
        merge_kernel,
        out_shape=[pltpu.HBM(x.shape, BF)] * 2,
        in_specs=[vmem()] * 5,
        out_specs=[vmem()] * 2,
        compiler_params=pltpu.CompilerParams(vmem_limit_bytes=8 * 2**20),
        name="merge_rows",
    )(x, *in_hbm(parts))


def in_hbm(arrays):
    return [pltpu.with_memory_space_constraint(a, pltpu.HBM) for a in arrays]


def load_kernel(*refs):
    n = len(refs) // 2
    copies = [pltpu.make_async_copy(refs[i], refs[n + i], refs[-1].at[i]) for i in range(n)]
    for copy in copies:
        copy.start()
    for copy in copies:
        copy.wait()


def load(arrays):
    return pl.pallas_call(
        load_kernel,
        out_shape=[pltpu.VMEM(a.shape, a.dtype) for a in arrays],
        in_specs=[anywhere()] * len(arrays),
        out_specs=[vmem()] * len(arrays),
        scratch_shapes=[pltpu.SemaphoreType.DMA((len(arrays),))],
        compiler_params=pltpu.CompilerParams(vmem_limit_bytes=4 * 2**20),
        cost_estimate=pl.CostEstimate(
            flops=0, bytes_accessed=2**24, transcendentals=0
        ),
        name="load",
    )(*in_hbm(arrays))


def softmax_rounded(scores):
    top = jnp.max(scores, axis=-1, keepdims=True)
    weights = jnp.exp(scores - top)
    return (weights / jnp.sum(weights, axis=-1, keepdims=True)).astype(BF)


NT = (((1,), (1,)), ((), ()))


PAIR = 768
HEADS = 4


def layer_kernel(place, cos_ref, sin_ref, *refs):
    *x_refs, w_ref = refs[: -SIDE - 6]
    outs = refs[-SIDE - 6 : -6]
    x_s, ctx_s, out_s, w_s, w_sem, o_sem = refs[-6:]
    groups = (pl.ds(0, PAIR), pl.ds(PAIR, PAIR), pl.ds(2 * PAIR, HEADS * HD))
    fetch = [
        pltpu.make_async_copy(w_ref.at[:, :, cut], w_s.at[:, :, cut], w_sem.at[i])
        for i, cut in enumerate(groups)
    ]
    for copy in fetch:
        copy.start()
    for i, ref in enumerate(x_refs):
        start = pl.multiple_of(place[i], 64)
        x_s[pl.ds(start, ref.shape[0])] = ref[...]
    rows, width = x_s.shape

    projected = []
    for half in range(2):
        fetch[half].wait()
        starts = [half * PAIR + 256 * i for i in range(3)]
        projected.append([
            jnp.dot(
                x_s[...], w_s[:, :, start : start + 256].reshape(width, 256),
                preferred_element_type=F32,
            )
            for start in starts
        ])
    fetch[2].wait()
    lower = lax.broadcasted_iota(jnp.int32, (rows, rows), 0) >= lax.broadcasted_iota(
        jnp.int32, (rows, rows), 1
    )
    cosine, sine = cos_ref[...], sin_ref[...]
    scale = 1.0 / jnp.sqrt(F32(HD))

    def turned(v):
        return (v * cosine + pltpu.roll(v, HD // 2, 1) * sine).astype(BF)

    for half, (q, k, v) in enumerate(projected):
        for head in range(2):
            cut = slice(head * HD, head * HD + HD)
            scores = lax.dot_general(
                turned(q[:, cut]), turned(k[:, cut]), NT, preferred_element_type=F32
            )
            weights = softmax_rounded(jnp.where(lower, scores * scale, -1e30))
            context = jnp.dot(weights, v[:, cut].astype(BF), preferred_element_type=F32)
            there = half * 256 + head * HD
            ctx_s[:, there : there + HD] = context.astype(BF)
    tile = 512
    for n in range(width // tile):
        chunks = slice(n * tile // 128, (n + 1) * tile // 128)
        total = lax.dot_general(
            ctx_s[...], w_s[chunks, :, 2 * PAIR :].reshape(tile, HEADS * HD), NT,
            preferred_element_type=F32,
        )
        out_s[:, n * tile : (n + 1) * tile] = total.astype(BF)
    copies = []
    for i, ref in enumerate(outs):
        start = pl.multiple_of(place[SIDE + i], 64)
        copies.append(pltpu.make_async_copy(out_s.at[pl.ds(start, 64)], ref, o_sem.at[i]))
        copies[-1].start()
    for copy in copies:
        copy.wait()


def layer(place, tables, blocks, weight):
    rows, width = sum(b.shape[0] for b in blocks), blocks[0].shape[1]
    return pl.pallas_call(
        layer_kernel,
        out_shape=[pltpu.HBM((64, width), BF)] * SIDE,
        in_specs=[smem()] + [vmem()] * (2 + len(blocks)) + [anywhere()],
        out_specs=[anywhere()] * SIDE,
        scratch_shapes=[
            pltpu.VMEM((rows, width), BF),
            pltpu.VMEM((rows, HEADS * HD), BF),
            pltpu.VMEM((rows, width), BF),
            pltpu.VMEM(weight.shape, BF),
            pltpu.SemaphoreType.DMA((3,)),
            pltpu.SemaphoreType.DMA((SIDE,)),
        ],
        compiler_params=pltpu.CompilerParams(vmem_limit_bytes=36 * 2**20),
        cost_estimate=pl.CostEstimate(
            flops=2 * rows * width * 2048, bytes_accessed=2**24, transcendentals=0
        ),
        name="layer",
    )(place, *tables, *in_hbm([*blocks, weight]))


TF = 16


def depth_kernel(x_ref, a_ref, b_ref, c_ref, d_ref, proj, dqkv, dout, logit, emb, target,
                 o_ref, u_s, qkv_s, ctx_s):
    new = summed(x_ref, a_ref, b_ref, c_ref, d_ref)
    normed = rms(new.astype(F32))
    depth_in = jnp.dot(normed, proj[...], preferred_element_type=F32).astype(BF)
    depth_in = depth_in.astype(F32)
    frames = x_ref.shape[0]
    streams = u_s.shape[0] // frames
    span = TF * streams
    for tile in range(frames // TF):
        base = depth_in[tile * TF : tile * TF + TF]
        for k in range(streams):
            cut = slice(tile * span + k * TF, tile * span + k * TF + TF)
            u_s[cut] = base + emb[cut].astype(F32)
    inputs = rms(u_s[...])
    for i in range(3):
        qkv_s[i] = jnp.dot(inputs, dqkv[i], preferred_element_type=F32).astype(BF)
    r = lax.broadcasted_iota(jnp.int32, (span, span), 0)
    q = lax.broadcasted_iota(jnp.int32, (span, span), 1)
    seen = ((r & (TF - 1)) == (q & (TF - 1))) & (r >= q)
    head_width = dout.shape[0]
    heads = head_width // HDD
    head = lax.broadcasted_iota(jnp.int32, (span, head_width), 1) // HDD
    seen = jnp.broadcast_to(seen[None], (heads, span, span)).reshape(heads * span, span)
    for tile in range(frames // TF):
        rows = slice(tile * span, tile * span + span)
        queries, keys, values = (qkv_s[i, rows] for i in range(3))
        queries = jnp.concatenate(
            [jnp.where(head == h, queries, jnp.zeros_like(queries)) for h in range(heads)]
        )
        scores = lax.dot_general(queries, keys, NT, preferred_element_type=F32)
        weights = softmax_rounded(jnp.where(seen, scores * HDD**-0.5, -1e30))
        context = jnp.dot(weights, values, preferred_element_type=F32)
        picked = context[:span]
        for h in range(1, heads):
            picked = jnp.where(head == h, context[h * span : (h + 1) * span], picked)
        ctx_s[rows] = picked.astype(BF)
    mixed = u_s[...] + jnp.dot(ctx_s[...], dout[...], preferred_element_type=F32)
    logits = jnp.dot(rms(mixed), logit[...], preferred_element_type=F32)
    top = jnp.max(logits, axis=-1, keepdims=True)
    total = jnp.sum(jnp.exp(logits - top), axis=-1, keepdims=True)
    entry = lax.broadcasted_iota(jnp.int32, logits.shape, 1)
    picked = jnp.sum(jnp.where(entry == target[...], logits, 0.0), axis=-1, keepdims=True)
    o_ref[...] = jnp.log(total) + top - picked


def depth(x, parts, proj, dqkv, dout, logit, emb, target):
    count, width = emb.shape
    head_width = dout.shape[0]
    return pl.pallas_call(
        depth_kernel,
        out_shape=jax.ShapeDtypeStruct((count, 1), F32),
        in_specs=[vmem()] * 11,
        out_specs=vmem(),
        scratch_shapes=[
            pltpu.VMEM((count, width), F32),
            pltpu.VMEM((3, count, head_width), BF),
            pltpu.VMEM((count, head_width), BF),
        ],
        compiler_params=pltpu.CompilerParams(vmem_limit_bytes=16 * 2**20),
        cost_estimate=pl.CostEstimate(
            flops=2 * count * width * 5120, bytes_accessed=2**22, transcendentals=0
        ),
        name="depth",
    )(x, *in_hbm(parts), proj, dqkv, dout, logit, emb, target)


def rope_tables(rows):
    half = HD // 2
    frequency = 10000.0 ** (-jnp.arange(half, dtype=F32) / half)
    angles = jnp.arange(rows).astype(F32)[:, None] * frequency[None, :]
    cosine, sine = jnp.cos(angles), jnp.sin(angles)
    return (
        jnp.concatenate([cosine, cosine], axis=1),
        jnp.concatenate([-sine, sine], axis=1),
    )


def packed_weights(qkv_weight, out_weight):
    w = jnp.transpose(qkv_weight[0], (1, 0, 2))
    o = out_weight[0]
    halves = []
    for i in range(2):
        cuts = [slice(512 * i + 256 * j, 512 * i + 256 * j + 256) for j in range(2)]
        parts = [w[k][:, cut] for cut in cuts for k in range(3)]
        halves.append(jnp.concatenate([*parts, o[512 * i : 512 * i + 512].T], axis=1))
    return jnp.stack(halves)


def local(
    frames_in, qkv_weight, out_weight, proj_weight, depth_qkv, depth_out, code_table,
    logit_weight, given_codes, given_delays,
):
    s = lax.axis_index("segment")
    f = lax.axis_index("frame")
    d = lax.axis_index("dp")
    row_count = frames_in.shape[1]
    part = row_count // 2
    streams = given_codes.shape[2]
    me = s * 2 + f

    def rows_of(i):
        i = i % SIDE
        return (i % 2) * row_count + (i // 2) * part

    sign = 1 - 2 * (d % 2)

    def place_of(starts):
        starts = (list(starts) + [0] * SIDE)[:SIDE]
        targets = [rows_of(me + k * sign + 4) for k in (0, 1, -1, 2)]
        return jnp.stack([*starts, *targets]).astype(jnp.int32)

    packed = packed_weights(qkv_weight, out_weight)
    kept = lax.dynamic_index_in_dim(packed, s, 0, keepdims=False)
    given = lax.dynamic_index_in_dim(packed, 1 - s, 0, keepdims=False)
    got = xswap(given, [(0, 3), (3, 0), (1, 2), (2, 1)])
    first = jnp.where(s == 0, kept, got)
    second = jnp.where(s == 0, got, kept)
    w0 = lax.all_gather(first, "dp")
    frames = frames_in[0]
    normed = norm_rows(frames)
    far = xhop(tied(normed, got), 1)

    given_tail = lax.ppermute(given_codes[0, row_count - DMAX :], "frame", [(0, 1)])

    def prepare(after):
        codes, delays = tied((given_codes, given_delays), after)
        tail = tied(given_tail, after)
        extended = jnp.concatenate([tail, codes[0]], axis=0)
        extended = lax.dynamic_slice_in_dim(extended, s * part, part + DMAX, 0)
        targets = extended[DMAX : DMAX + part]
        for lag in range(1, DMAX + 1):
            targets = jnp.where(
                delays[None, :] == lag, extended[DMAX - lag : DMAX - lag + part], targets
            )
        frame = rows_of(me) + jnp.arange(part, dtype=jnp.int32)
        is_valid = frame[:, None] >= delays[None, :]
        targets = jnp.clip(targets, 0, code_table.shape[0] - 1)

        def tiled(a):
            return jnp.transpose(a.reshape(part // TF, TF, streams), (0, 2, 1)).reshape(-1)

        def behind(a):
            return jnp.concatenate([jnp.zeros_like(a[:, :1]), a[:, :-1]], axis=1)

        emb = jnp.take(code_table, tiled(behind(targets)), axis=0, mode="clip")
        emb = jnp.where(tiled(behind(is_valid))[:, None], emb, jnp.zeros_like(emb))
        return emb, tiled(targets)[:, None], is_valid, rope_tables(2 * row_count)

    emb, target, is_valid, tables = prepare(far)
    w0, far, emb, target, tables, second = lax.optimization_barrier(
        (w0, far, emb, target, tables, second)
    )
    w1 = lax.all_gather(second, "dp")
    place0 = place_of([f * row_count, (1 - f) * row_count])
    sent = layer(place0, tables, [normed, far], w0)

    def spread(block):
        return [block, xhop(block, 1), xhop(block, -1), xhop2(block)]

    def scattered(sent):
        return [sent[0], xhop(sent[1], 1), xhop(sent[2], -1), xhop2(sent[3])]

    mine = lax.dynamic_slice_in_dim(frames, s * part, part, 0)
    x1, n1 = merge_rows(mine, scattered(sent))
    starts = [rows_of(me + k * sign + 4) for k in (0, -1, 1, 2)]
    sent = layer(place_of(starts), tables, spread(n1), w1)

    ready = [proj_weight, jnp.transpose(depth_qkv, (1, 0, 2)), depth_out, logit_weight]
    ready = load(tied(ready, sent))
    losses = depth(x1, scattered(sent), *ready, emb, target)
    losses = jnp.transpose(losses.reshape(part // TF, streams, TF), (0, 2, 1))
    losses = jnp.where(is_valid, losses.reshape(part, streams), 0.0)
    other = xhop2(losses)
    both = jnp.where(s == 0, jnp.stack([losses, other]), jnp.stack([other, losses]))
    return both.reshape(1, row_count, streams)


def solution(mesh):
    return jax.shard_map(
        local,
        mesh=mesh,
        in_specs=(
            P("dp", "frame", None),
            P("segment", "dp", None, "frame"),
            P("segment", "frame", "dp"),
            P(),
            P(),
            P(),
            P(),
            P(),
            P("dp", "frame", None),
            P(),
        ),
        out_specs=P("dp", "frame", None),
        check_vma=False,
    )
```

```python
import functools

import jax
import jax.numpy as jnp
from jax import lax
from jax.experimental import pallas as pl
from jax.experimental.pallas import tpu as pltpu
from jax.sharding import PartitionSpec as P

HD = 128
HDD = 64
DMAX = 2
ZN, YN = 4, 4
SIDE = 4
BF = jnp.bfloat16
F32 = jnp.float32
EPS = 1e-05


def xswap(value, pairs):
    return lax.ppermute(value, ("segment", "frame"), pairs)


def xhop(value, sign):
    pairs = []
    for d in range(2 * ZN * YN):
        step = sign * (1 - 2 * (d % 2))
        pairs += [(d * SIDE + i, d * SIDE + (i + step) % SIDE) for i in range(SIDE)]
    return lax.ppermute(value, ("dp", "segment", "frame"), pairs)


def tied(values, after):
    return lax.optimization_barrier((values, after))[0]


def xhop2(value):
    return xswap(value, [(i, (i + 2) % SIDE) for i in range(SIDE)])


def vmem():
    return pl.BlockSpec(memory_space=pltpu.VMEM)


def smem():
    return pl.BlockSpec(memory_space=pltpu.SMEM)


def anywhere():
    return pl.BlockSpec(memory_space=pl.ANY)


def rms(values):
    scale = lax.rsqrt(jnp.mean(values * values, axis=-1, keepdims=True) + EPS)
    return (values * scale).astype(BF)


def norm_kernel(x_ref, o_ref):
    o_ref[...] = rms(x_ref[...].astype(F32))


def norm_rows(x):
    return pl.pallas_call(
        norm_kernel,
        out_shape=pltpu.HBM(x.shape, BF),
        in_specs=[vmem()],
        out_specs=vmem(),
        compiler_params=pltpu.CompilerParams(vmem_limit_bytes=8 * 2**20),
        name="norm_rows",
    )(x)


def summed(*refs):
    total = refs[0][...].astype(F32)
    for ref in refs[1:]:
        total = total + ref[...].astype(F32)
    return total.astype(BF)


def merge_kernel(x_ref, a_ref, b_ref, c_ref, x_out, n_out):
    new = summed(x_ref, a_ref, b_ref, c_ref)
    x_out[...] = new
    n_out[...] = rms(new.astype(F32))


def merge_rows(x, parts):
    return pl.pallas_call(
        merge_kernel,
        out_shape=[pltpu.HBM(x.shape, BF)] * 2,
        in_specs=[vmem()] * 4,
        out_specs=[vmem()] * 2,
        compiler_params=pltpu.CompilerParams(vmem_limit_bytes=8 * 2**20),
        name="merge_rows",
    )(x, *parts)


def in_hbm(arrays):
    return [pltpu.with_memory_space_constraint(a, pltpu.HBM) for a in arrays]


def load_kernel(*refs):
    n = len(refs) // 2
    copies = [pltpu.make_async_copy(refs[i], refs[n + i], refs[-1].at[i]) for i in range(n)]
    for copy in copies:
        copy.start()
    for copy in copies:
        copy.wait()


def load(arrays):
    return pl.pallas_call(
        load_kernel,
        out_shape=[pltpu.VMEM(a.shape, a.dtype) for a in arrays],
        in_specs=[anywhere()] * len(arrays),
        out_specs=[vmem()] * len(arrays),
        scratch_shapes=[pltpu.SemaphoreType.DMA((len(arrays),))],
        compiler_params=pltpu.CompilerParams(vmem_limit_bytes=4 * 2**20),
        cost_estimate=pl.CostEstimate(
            flops=0, bytes_accessed=2**24, transcendentals=0
        ),
        name="load",
    )(*in_hbm(arrays))


def softmax_rounded(scores):
    top = jnp.max(scores, axis=-1, keepdims=True)
    weights = jnp.exp(scores - top)
    return (weights / jnp.sum(weights, axis=-1, keepdims=True)).astype(BF)


NT = (((1,), (1,)), ((), ()))


PAIR = 768
HEADS = 4
STEPS = 4


def layer_kernel(place, cos_ref, sin_ref, *refs):
    *x_refs, w_ref = refs[: -SIDE - 6]
    outs = refs[-SIDE - 6 : -6]
    x_s, ctx_s, out_s, w_s, w_sem, o_sem = refs[-6:]
    rows, width = x_s.shape
    count = w_s.shape[0] // STEPS
    fetch = [
        pltpu.make_async_copy(
            w_ref.at[pl.ds(i * count, count)], w_s.at[pl.ds(i * count, count)], w_sem.at[i]
        )
        for i in range(STEPS)
    ]
    for copy in fetch:
        copy.start()
    for i, ref in enumerate(x_refs):
        start = pl.multiple_of(place[i], 64)
        x_s[pl.ds(start, ref.shape[0])] = ref[...]

    def product(step, start):
        some = slice(step * count, (step + 1) * count)
        return jnp.dot(
            x_s[:, step * count * 128 : (step + 1) * count * 128],
            w_s[some, :, start : start + 256].reshape(count * 128, 256),
            preferred_element_type=F32,
        )

    projected = None
    for step, copy in enumerate(fetch):
        copy.wait()
        part = [
            [product(step, half * PAIR + 256 * i) for i in range(3)] for half in range(2)
        ]
        projected = part if step == 0 else [
            [a + b for a, b in zip(old, new)] for old, new in zip(projected, part)
        ]
    lower = lax.broadcasted_iota(jnp.int32, (rows, rows), 0) >= lax.broadcasted_iota(
        jnp.int32, (rows, rows), 1
    )
    cosine, sine = cos_ref[...], sin_ref[...]
    scale = 1.0 / jnp.sqrt(F32(HD))

    def turned(v):
        return (v * cosine + pltpu.roll(v, HD // 2, 1) * sine).astype(BF)

    for half, (q, k, v) in enumerate(projected):
        for head in range(2):
            cut = slice(head * HD, head * HD + HD)
            scores = lax.dot_general(
                turned(q[:, cut]), turned(k[:, cut]), NT, preferred_element_type=F32
            )
            weights = softmax_rounded(jnp.where(lower, scores * scale, -1e30))
            context = jnp.dot(weights, v[:, cut].astype(BF), preferred_element_type=F32)
            there = half * 256 + head * HD
            ctx_s[:, there : there + HD] = context.astype(BF)
    tile = 512
    for n in range(width // tile):
        chunks = slice(n * tile // 128, (n + 1) * tile // 128)
        total = lax.dot_general(
            ctx_s[...], w_s[chunks, :, 2 * PAIR :].reshape(tile, HEADS * HD), NT,
            preferred_element_type=F32,
        )
        out_s[:, n * tile : (n + 1) * tile] = total.astype(BF)
    copies = []
    for i, ref in enumerate(outs):
        start = pl.multiple_of(place[SIDE + i], 64)
        copies.append(pltpu.make_async_copy(out_s.at[pl.ds(start, 64)], ref, o_sem.at[i]))
        copies[-1].start()
    for copy in copies:
        copy.wait()


def layer(place, tables, blocks, weight):
    rows, width = sum(b.shape[0] for b in blocks), blocks[0].shape[1]
    return pl.pallas_call(
        layer_kernel,
        out_shape=[pltpu.HBM((64, width), BF)] * SIDE,
        in_specs=[smem()] + [vmem()] * (2 + len(blocks)) + [anywhere()],
        out_specs=[anywhere()] * SIDE,
        scratch_shapes=[
            pltpu.VMEM((rows, width), BF),
            pltpu.VMEM((rows, HEADS * HD), BF),
            pltpu.VMEM((rows, width), BF),
            pltpu.VMEM(weight.shape, BF),
            pltpu.SemaphoreType.DMA((STEPS,)),
            pltpu.SemaphoreType.DMA((SIDE,)),
        ],
        compiler_params=pltpu.CompilerParams(vmem_limit_bytes=36 * 2**20),
        cost_estimate=pl.CostEstimate(
            flops=2 * rows * width * 2048, bytes_accessed=2**24, transcendentals=0
        ),
        name="layer",
    )(place, *tables, *blocks, *in_hbm([weight]))


TF = 16


def depth_kernel(x_ref, a_ref, b_ref, c_ref, proj, dqkv, dout, logit, emb, target,
                 o_ref, u_s, qkv_s, ctx_s):
    new = summed(x_ref, a_ref, b_ref, c_ref)
    normed = rms(new.astype(F32))
    depth_in = jnp.dot(normed, proj[...], preferred_element_type=F32).astype(BF)
    depth_in = depth_in.astype(F32)
    frames = x_ref.shape[0]
    streams = u_s.shape[0] // frames
    span = TF * streams
    for tile in range(frames // TF):
        base = depth_in[tile * TF : tile * TF + TF]
        for k in range(streams):
            cut = slice(tile * span + k * TF, tile * span + k * TF + TF)
            u_s[cut] = base + emb[cut].astype(F32)
    inputs = rms(u_s[...])
    for i in range(3):
        qkv_s[i] = jnp.dot(inputs, dqkv[i], preferred_element_type=F32).astype(BF)
    r = lax.broadcasted_iota(jnp.int32, (span, span), 0)
    q = lax.broadcasted_iota(jnp.int32, (span, span), 1)
    seen = ((r & (TF - 1)) == (q & (TF - 1))) & (r >= q)
    head_width = dout.shape[0]
    heads = head_width // HDD
    head = lax.broadcasted_iota(jnp.int32, (span, head_width), 1) // HDD
    seen = jnp.broadcast_to(seen[None], (heads, span, span)).reshape(heads * span, span)
    for tile in range(frames // TF):
        rows = slice(tile * span, tile * span + span)
        queries, keys, values = (qkv_s[i, rows] for i in range(3))
        queries = jnp.concatenate(
            [jnp.where(head == h, queries, jnp.zeros_like(queries)) for h in range(heads)]
        )
        scores = lax.dot_general(queries, keys, NT, preferred_element_type=F32)
        weights = softmax_rounded(jnp.where(seen, scores * HDD**-0.5, -1e30))
        context = jnp.dot(weights, values, preferred_element_type=F32)
        picked = context[:span]
        for h in range(1, heads):
            picked = jnp.where(head == h, context[h * span : (h + 1) * span], picked)
        ctx_s[rows] = picked.astype(BF)
    mixed = u_s[...] + jnp.dot(ctx_s[...], dout[...], preferred_element_type=F32)
    logits = jnp.dot(rms(mixed), logit[...], preferred_element_type=F32)
    top = jnp.max(logits, axis=-1, keepdims=True)
    total = jnp.sum(jnp.exp(logits - top), axis=-1, keepdims=True)
    entry = lax.broadcasted_iota(jnp.int32, logits.shape, 1)
    picked = jnp.sum(jnp.where(entry == target[...], logits, 0.0), axis=-1, keepdims=True)
    o_ref[...] = jnp.log(total) + top - picked


def depth(x, parts, proj, dqkv, dout, logit, emb, target):
    count, width = emb.shape
    head_width = dout.shape[0]
    return pl.pallas_call(
        depth_kernel,
        out_shape=jax.ShapeDtypeStruct((count, 1), F32),
        in_specs=[vmem()] * 10,
        out_specs=vmem(),
        scratch_shapes=[
            pltpu.VMEM((count, width), F32),
            pltpu.VMEM((3, count, head_width), BF),
            pltpu.VMEM((count, head_width), BF),
        ],
        compiler_params=pltpu.CompilerParams(vmem_limit_bytes=16 * 2**20),
        cost_estimate=pl.CostEstimate(
            flops=2 * count * width * 5120, bytes_accessed=2**22, transcendentals=0
        ),
        name="depth",
    )(x, *parts, proj, dqkv, dout, logit, emb, target)


def rope_tables(rows):
    half = HD // 2
    frequency = 10000.0 ** (-jnp.arange(half, dtype=F32) / half)
    angles = jnp.arange(rows).astype(F32)[:, None] * frequency[None, :]
    cosine, sine = jnp.cos(angles), jnp.sin(angles)
    return (
        jnp.concatenate([cosine, cosine], axis=1),
        jnp.concatenate([-sine, sine], axis=1),
    )


def packed_weights(qkv_weight, out_weight):
    w = jnp.transpose(qkv_weight[0], (1, 0, 2))
    o = out_weight[0]
    halves = []
    for i in range(2):
        cuts = [slice(512 * i + 256 * j, 512 * i + 256 * j + 256) for j in range(2)]
        parts = [w[k][:, cut] for cut in cuts for k in range(3)]
        halves.append(jnp.concatenate([*parts, o[512 * i : 512 * i + 512].T], axis=1))
    return jnp.stack(halves)


def local(
    frames_in, qkv_weight, out_weight, proj_weight, depth_qkv, depth_out, code_table,
    logit_weight, given_codes, given_delays,
):
    s = lax.axis_index("segment")
    f = lax.axis_index("frame")
    d = lax.axis_index("dp")
    row_count = frames_in.shape[1]
    part = row_count // 2
    streams = given_codes.shape[2]
    me = s * 2 + f

    def rows_of(i):
        i = i % SIDE
        return (i % 2) * row_count + (i // 2) * part

    sign = 1 - 2 * (d % 2)

    def place_of(starts):
        starts = (list(starts) + [0] * SIDE)[:SIDE]
        targets = [rows_of(me + k * sign + 4) for k in (0, 1, -1, 2)]
        return jnp.stack([*starts, *targets]).astype(jnp.int32)

    packed = packed_weights(qkv_weight, out_weight)
    kept = lax.dynamic_index_in_dim(packed, s, 0, keepdims=False)
    given = lax.dynamic_index_in_dim(packed, 1 - s, 0, keepdims=False)
    got = xswap(given, [(0, 3), (3, 0), (1, 2), (2, 1)])
    first = jnp.where(s == 0, kept, got)
    w0 = lax.all_gather(first, "dp")
    frames = frames_in[0]
    normed = norm_rows(frames)
    far = xhop(tied(normed, got), 1)

    given_tail = lax.ppermute(given_codes[0, row_count - DMAX :], "frame", [(0, 1)])

    def prepare(after):
        codes, delays = tied((given_codes, given_delays), after)
        tail = tied(given_tail, after)
        extended = jnp.concatenate([tail, codes[0]], axis=0)
        extended = lax.dynamic_slice_in_dim(extended, s * part, part + DMAX, 0)
        targets = extended[DMAX : DMAX + part]
        for lag in range(1, DMAX + 1):
            targets = jnp.where(
                delays[None, :] == lag, extended[DMAX - lag : DMAX - lag + part], targets
            )
        frame = rows_of(me) + jnp.arange(part, dtype=jnp.int32)
        is_valid = frame[:, None] >= delays[None, :]
        targets = jnp.clip(targets, 0, code_table.shape[0] - 1)

        def tiled(a):
            return jnp.transpose(a.reshape(part // TF, TF, streams), (0, 2, 1)).reshape(-1)

        def behind(a):
            return jnp.concatenate([jnp.zeros_like(a[:, :1]), a[:, :-1]], axis=1)

        emb = jnp.take(code_table, tiled(behind(targets)), axis=0, mode="clip")
        emb = jnp.where(tiled(behind(is_valid))[:, None], emb, jnp.zeros_like(emb))
        return emb, tiled(targets)[:, None], is_valid, rope_tables(2 * row_count)

    emb, target, is_valid, tables = prepare(far)
    far, emb, target, tables, (kept, got) = lax.optimization_barrier(
        (far, emb, target, tables, (kept, got))
    )
    w1 = lax.all_gather(jnp.where(s == 0, got, kept), "dp")
    place0 = place_of([f * row_count, (1 - f) * row_count])
    sent = layer(place0, tables, [normed, far], w0)

    def spread(block):
        return [block, xhop(block, 1), xhop(block, -1), xhop2(block)]

    def scattered(sent):
        relayed, back = xhop(sent[3], 1), xhop(sent[2], -1)
        relayed = (sent[1].astype(F32) + relayed.astype(F32)).astype(BF)
        return [sent[0], xhop(relayed, 1), back]

    mine = lax.dynamic_slice_in_dim(frames, s * part, part, 0)
    x1, n1 = merge_rows(mine, scattered(sent))
    starts = [rows_of(me + k * sign + 4) for k in (0, -1, 1, 2)]
    sent = layer(place_of(starts), tables, spread(n1), w1)

    ready = [proj_weight, jnp.transpose(depth_qkv, (1, 0, 2)), depth_out, logit_weight]
    ready = load(tied(ready, sent))
    losses = depth(x1, scattered(sent), *ready, emb, target)
    losses = jnp.transpose(losses.reshape(part // TF, streams, TF), (0, 2, 1))
    losses = jnp.where(is_valid, losses.reshape(part, streams), 0.0)
    other = xhop2(losses)
    both = jnp.where(s == 0, jnp.stack([losses, other]), jnp.stack([other, losses]))
    return both.reshape(1, row_count, streams)


def solution(mesh):
    return jax.shard_map(
        local,
        mesh=mesh,
        in_specs=(
            P("dp", "frame", None),
            P("segment", "dp", None, "frame"),
            P("segment", "frame", "dp"),
            P(),
            P(),
            P(),
            P(),
            P(),
            P("dp", "frame", None),
            P(),
        ),
        out_specs=P("dp", "frame", None),
        check_vma=False,
    )
```

```python
import functools

import jax
import jax.numpy as jnp
from jax import lax
from jax.experimental import pallas as pl
from jax.experimental.pallas import tpu as pltpu
from jax.sharding import PartitionSpec as P

HD = 128
HDD = 64
DMAX = 2
ZN, YN = 4, 4
SIDE = 4
BF = jnp.bfloat16
F32 = jnp.float32
EPS = 1e-05


def xswap(value, pairs):
    return lax.ppermute(value, ("segment", "frame"), pairs)


def xhop(value, sign):
    pairs = []
    for d in range(2 * ZN * YN):
        step = sign * (1 - 2 * (d % 2))
        pairs += [(d * SIDE + i, d * SIDE + (i + step) % SIDE) for i in range(SIDE)]
    return lax.ppermute(value, ("dp", "segment", "frame"), pairs)


def tied(values, after):
    return lax.optimization_barrier((values, after))[0]


def xhop2(value):
    return xswap(value, [(i, (i + 2) % SIDE) for i in range(SIDE)])


def vmem():
    return pl.BlockSpec(memory_space=pltpu.VMEM)


def smem():
    return pl.BlockSpec(memory_space=pltpu.SMEM)


def anywhere():
    return pl.BlockSpec(memory_space=pl.ANY)


def rms(values):
    scale = lax.rsqrt(jnp.mean(values * values, axis=-1, keepdims=True) + EPS)
    return (values * scale).astype(BF)


def norm_kernel(x_ref, o_ref):
    o_ref[...] = rms(x_ref[...].astype(F32))


def norm_rows(x):
    return pl.pallas_call(
        norm_kernel,
        out_shape=pltpu.HBM(x.shape, BF),
        in_specs=[vmem()],
        out_specs=vmem(),
        compiler_params=pltpu.CompilerParams(vmem_limit_bytes=8 * 2**20),
        name="norm_rows",
    )(x)


def summed(*refs):
    total = refs[0][...].astype(F32)
    for ref in refs[1:]:
        total = total + ref[...].astype(F32)
    return total.astype(BF)


def merge_kernel(x_ref, a_ref, b_ref, c_ref, x_out, n_out):
    new = summed(x_ref, a_ref, b_ref, c_ref)
    x_out[...] = new
    n_out[...] = rms(new.astype(F32))


def merge_rows(x, parts):
    return pl.pallas_call(
        merge_kernel,
        out_shape=[pltpu.HBM(x.shape, BF), pltpu.VMEM(x.shape, BF)],
        in_specs=[vmem()] * 4,
        out_specs=[vmem()] * 2,
        compiler_params=pltpu.CompilerParams(vmem_limit_bytes=8 * 2**20),
        name="merge_rows",
    )(x, *parts)


def in_hbm(arrays):
    return [pltpu.with_memory_space_constraint(a, pltpu.HBM) for a in arrays]


def load_kernel(*refs):
    n = len(refs) // 2
    copies = [pltpu.make_async_copy(refs[i], refs[n + i], refs[-1].at[i]) for i in range(n)]
    for copy in copies:
        copy.start()
    for copy in copies:
        copy.wait()


def load(arrays):
    return pl.pallas_call(
        load_kernel,
        out_shape=[pltpu.VMEM(a.shape, a.dtype) for a in arrays],
        in_specs=[anywhere()] * len(arrays),
        out_specs=[vmem()] * len(arrays),
        scratch_shapes=[pltpu.SemaphoreType.DMA((len(arrays),))],
        compiler_params=pltpu.CompilerParams(vmem_limit_bytes=4 * 2**20),
        cost_estimate=pl.CostEstimate(
            flops=0, bytes_accessed=2**24, transcendentals=0
        ),
        name="load",
    )(*in_hbm(arrays))


def softmax_rounded(scores):
    top = jnp.max(scores, axis=-1, keepdims=True)
    weights = jnp.exp(scores - top)
    return (weights / jnp.sum(weights, axis=-1, keepdims=True)).astype(BF)


NT = (((1,), (1,)), ((), ()))


PAIR = 768
HEADS = 4
STEPS = 8


def layer_kernel(place, cos_ref, sin_ref, *refs):
    *x_refs, w_ref = refs[: -SIDE - 6]
    outs = refs[-SIDE - 6 : -6]
    x_s, ctx_s, out_s, w_s, w_sem, o_sem = refs[-6:]
    rows, width = x_s.shape
    count = w_s.shape[0] // STEPS
    fetch = [
        pltpu.make_async_copy(
            w_ref.at[pl.ds(i * count, count)], w_s.at[pl.ds(i * count, count)], w_sem.at[i]
        )
        for i in range(STEPS)
    ]
    for copy in fetch:
        copy.start()
    for i, ref in enumerate(x_refs):
        start = pl.multiple_of(place[i], 64)
        x_s[pl.ds(start, ref.shape[0])] = ref[...]

    def product(step, start):
        some = slice(step * count, (step + 1) * count)
        return jnp.dot(
            x_s[:, step * count * 128 : (step + 1) * count * 128],
            w_s[some, :, start : start + 256].reshape(count * 128, 256),
            preferred_element_type=F32,
        )

    projected = None
    for step, copy in enumerate(fetch):
        copy.wait()
        part = [
            [product(step, half * PAIR + 256 * i) for i in range(3)] for half in range(2)
        ]
        projected = part if step == 0 else [
            [a + b for a, b in zip(old, new)] for old, new in zip(projected, part)
        ]
    lower = lax.broadcasted_iota(jnp.int32, (rows, rows), 0) >= lax.broadcasted_iota(
        jnp.int32, (rows, rows), 1
    )
    cosine, sine = cos_ref[...], sin_ref[...]
    scale = 1.0 / jnp.sqrt(F32(HD))

    def turned(v):
        return (v * cosine + pltpu.roll(v, HD // 2, 1) * sine).astype(BF)

    for half, (q, k, v) in enumerate(projected):
        for head in range(2):
            cut = slice(head * HD, head * HD + HD)
            scores = lax.dot_general(
                turned(q[:, cut]), turned(k[:, cut]), NT, preferred_element_type=F32
            )
            weights = softmax_rounded(jnp.where(lower, scores * scale, -1e30))
            context = jnp.dot(weights, v[:, cut].astype(BF), preferred_element_type=F32)
            there = half * 256 + head * HD
            ctx_s[:, there : there + HD] = context.astype(BF)
    tile = 512
    for n in range(width // tile):
        chunks = slice(n * tile // 128, (n + 1) * tile // 128)
        total = lax.dot_general(
            ctx_s[...], w_s[chunks, :, 2 * PAIR :].reshape(tile, HEADS * HD), NT,
            preferred_element_type=F32,
        )
        out_s[:, n * tile : (n + 1) * tile] = total.astype(BF)
    copies = []
    for i, ref in enumerate(outs):
        start = pl.multiple_of(place[SIDE + i], 64)
        copies.append(pltpu.make_async_copy(out_s.at[pl.ds(start, 64)], ref, o_sem.at[i]))
        copies[-1].start()
    for copy in copies:
        copy.wait()


def layer(place, tables, blocks, weight):
    rows, width = sum(b.shape[0] for b in blocks), blocks[0].shape[1]
    return pl.pallas_call(
        layer_kernel,
        out_shape=[pltpu.HBM((64, width), BF)] * SIDE,
        in_specs=[smem()] + [vmem()] * (2 + len(blocks)) + [anywhere()],
        out_specs=[anywhere()] * SIDE,
        scratch_shapes=[
            pltpu.VMEM((rows, width), BF),
            pltpu.VMEM((rows, HEADS * HD), BF),
            pltpu.VMEM((rows, width), BF),
            pltpu.VMEM(weight.shape, BF),
            pltpu.SemaphoreType.DMA((STEPS,)),
            pltpu.SemaphoreType.DMA((SIDE,)),
        ],
        compiler_params=pltpu.CompilerParams(vmem_limit_bytes=36 * 2**20),
        cost_estimate=pl.CostEstimate(
            flops=2 * rows * width * 2048, bytes_accessed=2**24, transcendentals=0
        ),
        name="layer",
    )(place, *tables, *blocks, *in_hbm([weight]))


TF = 16


def depth_kernel(x_ref, a_ref, b_ref, c_ref, proj, dqkv, dout, logit, emb, target,
                 o_ref, u_s, qkv_s, ctx_s):
    new = summed(x_ref, a_ref, b_ref, c_ref)
    normed = rms(new.astype(F32))
    depth_in = jnp.dot(normed, proj[...], preferred_element_type=F32).astype(BF)
    depth_in = depth_in.astype(F32)
    frames = x_ref.shape[0]
    streams = u_s.shape[0] // frames
    span = TF * streams
    for tile in range(frames // TF):
        base = depth_in[tile * TF : tile * TF + TF]
        for k in range(streams):
            cut = slice(tile * span + k * TF, tile * span + k * TF + TF)
            u_s[cut] = base + emb[cut].astype(F32)
    inputs = rms(u_s[...])
    for i in range(3):
        qkv_s[i] = jnp.dot(inputs, dqkv[i], preferred_element_type=F32).astype(BF)
    r = lax.broadcasted_iota(jnp.int32, (span, span), 0)
    q = lax.broadcasted_iota(jnp.int32, (span, span), 1)
    seen = ((r & (TF - 1)) == (q & (TF - 1))) & (r >= q)
    head_width = dout.shape[0]
    heads = head_width // HDD
    head = lax.broadcasted_iota(jnp.int32, (span, head_width), 1) // HDD
    seen = jnp.broadcast_to(seen[None], (heads, span, span)).reshape(heads * span, span)
    for tile in range(frames // TF):
        rows = slice(tile * span, tile * span + span)
        queries, keys, values = (qkv_s[i, rows] for i in range(3))
        queries = jnp.concatenate(
            [jnp.where(head == h, queries, jnp.zeros_like(queries)) for h in range(heads)]
        )
        scores = lax.dot_general(queries, keys, NT, preferred_element_type=F32)
        weights = softmax_rounded(jnp.where(seen, scores * HDD**-0.5, -1e30))
        context = jnp.dot(weights, values, preferred_element_type=F32)
        picked = context[:span]
        for h in range(1, heads):
            picked = jnp.where(head == h, context[h * span : (h + 1) * span], picked)
        ctx_s[rows] = picked.astype(BF)
    mixed = u_s[...] + jnp.dot(ctx_s[...], dout[...], preferred_element_type=F32)
    logits = jnp.dot(rms(mixed), logit[...], preferred_element_type=F32)
    top = jnp.max(logits, axis=-1, keepdims=True)
    total = jnp.sum(jnp.exp(logits - top), axis=-1, keepdims=True)
    entry = lax.broadcasted_iota(jnp.int32, logits.shape, 1)
    picked = jnp.sum(jnp.where(entry == target[...], logits, 0.0), axis=-1, keepdims=True)
    o_ref[...] = jnp.log(total) + top - picked


def depth(x, parts, proj, dqkv, dout, logit, emb, target):
    count, width = emb.shape
    head_width = dout.shape[0]
    return pl.pallas_call(
        depth_kernel,
        out_shape=jax.ShapeDtypeStruct((count, 1), F32),
        in_specs=[vmem()] * 10,
        out_specs=vmem(),
        scratch_shapes=[
            pltpu.VMEM((count, width), F32),
            pltpu.VMEM((3, count, head_width), BF),
            pltpu.VMEM((count, head_width), BF),
        ],
        compiler_params=pltpu.CompilerParams(vmem_limit_bytes=16 * 2**20),
        cost_estimate=pl.CostEstimate(
            flops=2 * count * width * 5120, bytes_accessed=2**22, transcendentals=0
        ),
        name="depth",
    )(x, *parts, proj, dqkv, dout, logit, emb, target)


def rope_tables(rows):
    half = HD // 2
    frequency = 10000.0 ** (-jnp.arange(half, dtype=F32) / half)
    angles = jnp.arange(rows).astype(F32)[:, None] * frequency[None, :]
    cosine, sine = jnp.cos(angles), jnp.sin(angles)
    return (
        jnp.concatenate([cosine, cosine], axis=1),
        jnp.concatenate([-sine, sine], axis=1),
    )


def packed_qkv(qkv_weight):
    w = jnp.transpose(qkv_weight[0], (1, 0, 2))
    halves = []
    for i in range(2):
        cuts = [slice(512 * i + 256 * j, 512 * i + 256 * j + 256) for j in range(2)]
        halves.append(jnp.concatenate([w[k][:, cut] for cut in cuts for k in range(3)], axis=1))
    return jnp.stack(halves)


def packed_out(out_weight):
    o = out_weight[0]
    return jnp.stack([o[512 * i : 512 * i + 512].T for i in range(2)])


def local(
    frames_in, qkv_weight, out_weight, proj_weight, depth_qkv, depth_out, code_table,
    logit_weight, given_codes, given_delays,
):
    s = lax.axis_index("segment")
    f = lax.axis_index("frame")
    d = lax.axis_index("dp")
    row_count = frames_in.shape[1]
    part = row_count // 2
    streams = given_codes.shape[2]
    me = s * 2 + f

    def rows_of(i):
        i = i % SIDE
        return (i % 2) * row_count + (i // 2) * part

    sign = 1 - 2 * (d % 2)

    def place_of(starts):
        starts = (list(starts) + [0] * SIDE)[:SIDE]
        targets = [rows_of(me + k * sign + 4) for k in (0, 1, -1, 2)]
        return jnp.stack([*starts, *targets]).astype(jnp.int32)

    kept, got = [], []
    for packed in (packed_qkv(qkv_weight), packed_out(out_weight)):
        kept.append(lax.dynamic_index_in_dim(packed, s, 0, keepdims=False))
        given = lax.dynamic_index_in_dim(packed, 1 - s, 0, keepdims=False)
        got.append(xswap(given, [(0, 3), (3, 0), (1, 2), (2, 1)]))
    kept, got = (jnp.concatenate(parts, axis=1) for parts in (kept, got))
    first = jnp.where(s == 0, kept, got)
    w0 = lax.all_gather(first, "dp")
    frames = frames_in[0]
    normed = norm_rows(frames)
    far = xhop(tied(normed, got), 1)

    given_tail = lax.ppermute(given_codes[0, row_count - DMAX :], "frame", [(0, 1)])

    def prepare(after):
        codes, delays = tied((given_codes, given_delays), after)
        tail = tied(given_tail, after)
        extended = jnp.concatenate([tail, codes[0]], axis=0)
        extended = lax.dynamic_slice_in_dim(extended, s * part, part + DMAX, 0)
        targets = extended[DMAX : DMAX + part]
        for lag in range(1, DMAX + 1):
            targets = jnp.where(
                delays[None, :] == lag, extended[DMAX - lag : DMAX - lag + part], targets
            )
        frame = rows_of(me) + jnp.arange(part, dtype=jnp.int32)
        is_valid = frame[:, None] >= delays[None, :]
        targets = jnp.clip(targets, 0, code_table.shape[0] - 1)

        def tiled(a):
            return jnp.transpose(a.reshape(part // TF, TF, streams), (0, 2, 1)).reshape(-1)

        def behind(a):
            return jnp.concatenate([jnp.zeros_like(a[:, :1]), a[:, :-1]], axis=1)

        emb = jnp.take(code_table, tiled(behind(targets)), axis=0, mode="clip")
        emb = jnp.where(tiled(behind(is_valid))[:, None], emb, jnp.zeros_like(emb))
        return emb, tiled(targets)[:, None], is_valid, rope_tables(2 * row_count)

    emb, target, is_valid, tables = prepare(far)
    far, emb, target, tables, (kept, got) = lax.optimization_barrier(
        (far, emb, target, tables, (kept, got))
    )
    w1 = lax.all_gather(jnp.where(s == 0, got, kept), "dp")
    place0 = place_of([f * row_count, (1 - f) * row_count])
    sent = layer(place0, tables, [normed, far], w0)

    def spread(block):
        return [block, xhop(block, 1), xhop(block, -1), xhop2(block)]

    def scattered(sent):
        relayed, back = xhop(sent[3], 1), xhop(sent[2], -1)
        relayed = (sent[1].astype(F32) + relayed.astype(F32)).astype(BF)
        return [sent[0], xhop(relayed, 1), back]

    mine = lax.dynamic_slice_in_dim(frames, s * part, part, 0)
    x1, n1 = merge_rows(mine, scattered(sent))
    starts = [rows_of(me + k * sign + 4) for k in (0, -1, 1, 2)]
    sent = layer(place_of(starts), tables, spread(n1), w1)

    ready = [proj_weight, jnp.transpose(depth_qkv, (1, 0, 2)), depth_out, logit_weight]
    ready = load(tied(ready, sent))
    losses = depth(x1, scattered(sent), *ready, emb, target)
    losses = jnp.transpose(losses.reshape(part // TF, streams, TF), (0, 2, 1))
    losses = jnp.where(is_valid, losses.reshape(part, streams), 0.0)
    other = xhop2(losses)
    both = jnp.where(s == 0, jnp.stack([losses, other]), jnp.stack([other, losses]))
    return both.reshape(1, row_count, streams)


def solution(mesh):
    return jax.shard_map(
        local,
        mesh=mesh,
        in_specs=(
            P("dp", "frame", None),
            P("segment", "dp", None, "frame"),
            P("segment", "frame", "dp"),
            P(),
            P(),
            P(),
            P(),
            P(),
            P("dp", "frame", None),
            P(),
        ),
        out_specs=P("dp", "frame", None),
        check_vma=False,
    )
```

```python
import functools

import jax
import jax.numpy as jnp
from jax import lax
from jax.experimental import pallas as pl
from jax.experimental.pallas import tpu as pltpu
from jax.sharding import PartitionSpec as P

HD = 128
HDD = 64
DMAX = 2
ZN, YN = 4, 4
SIDE = 4
BF = jnp.bfloat16
F32 = jnp.float32
EPS = 1e-05


def xswap(value, pairs):
    return lax.ppermute(value, ("segment", "frame"), pairs)


def xhop(value, sign):
    pairs = []
    for d in range(2 * ZN * YN):
        step = sign * (1 - 2 * (d % 2))
        pairs += [(d * SIDE + i, d * SIDE + (i + step) % SIDE) for i in range(SIDE)]
    return lax.ppermute(value, ("dp", "segment", "frame"), pairs)


def tied(values, after):
    return lax.optimization_barrier((values, after))[0]


def xhop2(value):
    return xswap(value, [(i, (i + 2) % SIDE) for i in range(SIDE)])


def vmem():
    return pl.BlockSpec(memory_space=pltpu.VMEM)


def smem():
    return pl.BlockSpec(memory_space=pltpu.SMEM)


def anywhere():
    return pl.BlockSpec(memory_space=pl.ANY)


def rms(values):
    scale = lax.rsqrt(jnp.mean(values * values, axis=-1, keepdims=True) + EPS)
    return (values * scale).astype(BF)


def norm_kernel(x_ref, o_ref):
    o_ref[...] = rms(x_ref[...].astype(F32))


def norm_rows(x):
    return pl.pallas_call(
        norm_kernel,
        out_shape=pltpu.HBM(x.shape, BF),
        in_specs=[vmem()],
        out_specs=vmem(),
        compiler_params=pltpu.CompilerParams(vmem_limit_bytes=8 * 2**20),
        name="norm_rows",
    )(x)


def summed(*refs):
    total = refs[0][...].astype(F32)
    for ref in refs[1:]:
        total = total + ref[...].astype(F32)
    return total.astype(BF)


def merge_kernel(x_ref, a_ref, b_ref, c_ref, x_out, n_out):
    new = summed(x_ref, a_ref, b_ref, c_ref)
    x_out[...] = new
    n_out[...] = rms(new.astype(F32))


def merge_rows(x, parts):
    return pl.pallas_call(
        merge_kernel,
        out_shape=[pltpu.HBM(x.shape, BF), pltpu.VMEM(x.shape, BF)],
        in_specs=[vmem()] * 4,
        out_specs=[vmem()] * 2,
        compiler_params=pltpu.CompilerParams(vmem_limit_bytes=8 * 2**20),
        name="merge_rows",
    )(x, *parts)


def in_hbm(arrays):
    return [pltpu.with_memory_space_constraint(a, pltpu.HBM) for a in arrays]


def load_kernel(*refs):
    n = len(refs) // 2
    copies = [pltpu.make_async_copy(refs[i], refs[n + i], refs[-1].at[i]) for i in range(n)]
    for copy in copies:
        copy.start()
    for copy in copies:
        copy.wait()


def load(arrays):
    return pl.pallas_call(
        load_kernel,
        out_shape=[pltpu.VMEM(a.shape, a.dtype) for a in arrays],
        in_specs=[anywhere()] * len(arrays),
        out_specs=[vmem()] * len(arrays),
        scratch_shapes=[pltpu.SemaphoreType.DMA((len(arrays),))],
        compiler_params=pltpu.CompilerParams(vmem_limit_bytes=4 * 2**20),
        cost_estimate=pl.CostEstimate(
            flops=0, bytes_accessed=2**24, transcendentals=0
        ),
        name="load",
    )(*in_hbm(arrays))


def softmax_rounded(scores):
    top = jnp.max(scores, axis=-1, keepdims=True)
    weights = jnp.exp(scores - top)
    return (weights / jnp.sum(weights, axis=-1, keepdims=True)).astype(BF)


NT = (((1,), (1,)), ((), ()))


PAIR = 768
HEADS = 4
STEPS = 8


def layer_kernel(place, cos_ref, sin_ref, *refs):
    *x_refs, w_ref = refs[: -SIDE - 6]
    outs = refs[-SIDE - 6 : -6]
    x_s, ctx_s, out_s, w_s, w_sem, o_sem = refs[-6:]
    rows, width = x_s.shape
    count = w_s.shape[0] // STEPS
    fetch = [
        pltpu.make_async_copy(
            w_ref.at[pl.ds(i * count, count)], w_s.at[pl.ds(i * count, count)], w_sem.at[i]
        )
        for i in range(STEPS)
    ]
    for copy in fetch:
        copy.start()
    for i, ref in enumerate(x_refs):
        start = pl.multiple_of(place[i], 64)
        x_s[pl.ds(start, ref.shape[0])] = ref[...]

    def product(step, start):
        some = slice(step * count, (step + 1) * count)
        return jnp.dot(
            x_s[:, step * count * 128 : (step + 1) * count * 128],
            w_s[some, :, start : start + 256].reshape(count * 128, 256),
            preferred_element_type=F32,
        )

    projected = None
    for step, copy in enumerate(fetch):
        copy.wait()
        part = [
            [product(step, half * PAIR + 256 * i) for i in range(3)] for half in range(2)
        ]
        projected = part if step == 0 else [
            [a + b for a, b in zip(old, new)] for old, new in zip(projected, part)
        ]
    lower = lax.broadcasted_iota(jnp.int32, (rows, rows), 0) >= lax.broadcasted_iota(
        jnp.int32, (rows, rows), 1
    )
    cosine, sine = cos_ref[...], sin_ref[...]
    scale = 1.0 / jnp.sqrt(F32(HD))

    def turned(v):
        return (v * cosine + pltpu.roll(v, HD // 2, 1) * sine).astype(BF)

    for half, (q, k, v) in enumerate(projected):
        for head in range(2):
            cut = slice(head * HD, head * HD + HD)
            scores = lax.dot_general(
                turned(q[:, cut]), turned(k[:, cut]), NT, preferred_element_type=F32
            )
            weights = softmax_rounded(jnp.where(lower, scores * scale, -1e30))
            context = jnp.dot(weights, v[:, cut].astype(BF), preferred_element_type=F32)
            there = half * 256 + head * HD
            ctx_s[:, there : there + HD] = context.astype(BF)
    tile = 512
    for n in range(width // tile):
        chunks = slice(n * tile // 128, (n + 1) * tile // 128)
        total = lax.dot_general(
            ctx_s[...], w_s[chunks, :, 2 * PAIR :].reshape(tile, HEADS * HD), NT,
            preferred_element_type=F32,
        )
        out_s[:, n * tile : (n + 1) * tile] = total.astype(BF)
    copies = []
    for i, ref in enumerate(outs):
        start = pl.multiple_of(place[SIDE + i], 64)
        copies.append(pltpu.make_async_copy(out_s.at[pl.ds(start, 64)], ref, o_sem.at[i]))
        copies[-1].start()
    for copy in copies:
        copy.wait()


def layer(place, tables, blocks, weight):
    rows, width = sum(b.shape[0] for b in blocks), blocks[0].shape[1]
    return pl.pallas_call(
        layer_kernel,
        out_shape=[pltpu.VMEM((64, width), BF)] * SIDE,
        in_specs=[smem()] + [vmem()] * (2 + len(blocks)) + [anywhere()],
        out_specs=[vmem()] * SIDE,
        scratch_shapes=[
            pltpu.VMEM((rows, width), BF),
            pltpu.VMEM((rows, HEADS * HD), BF),
            pltpu.VMEM((rows, width), BF),
            pltpu.VMEM(weight.shape, BF),
            pltpu.SemaphoreType.DMA((STEPS,)),
            pltpu.SemaphoreType.DMA((SIDE,)),
        ],
        compiler_params=pltpu.CompilerParams(vmem_limit_bytes=28 * 2**20),
        cost_estimate=pl.CostEstimate(
            flops=2 * rows * width * 2048, bytes_accessed=2**24, transcendentals=0
        ),
        name="layer",
    )(place, *tables, *blocks, *in_hbm([weight]))


TF = 16


def depth_kernel(x_ref, a_ref, b_ref, c_ref, proj, dqkv, dout, logit, emb, target,
                 o_ref, u_s, qkv_s, ctx_s):
    new = summed(x_ref, a_ref, b_ref, c_ref)
    normed = rms(new.astype(F32))
    depth_in = jnp.dot(normed, proj[...], preferred_element_type=F32).astype(BF)
    depth_in = depth_in.astype(F32)
    frames = x_ref.shape[0]
    streams = u_s.shape[0] // frames
    span = TF * streams
    for tile in range(frames // TF):
        base = depth_in[tile * TF : tile * TF + TF]
        for k in range(streams):
            cut = slice(tile * span + k * TF, tile * span + k * TF + TF)
            u_s[cut] = base + emb[cut].astype(F32)
    inputs = rms(u_s[...])
    for i in range(3):
        qkv_s[i] = jnp.dot(inputs, dqkv[i], preferred_element_type=F32).astype(BF)
    r = lax.broadcasted_iota(jnp.int32, (span, span), 0)
    q = lax.broadcasted_iota(jnp.int32, (span, span), 1)
    seen = ((r & (TF - 1)) == (q & (TF - 1))) & (r >= q)
    head_width = dout.shape[0]
    heads = head_width // HDD
    head = lax.broadcasted_iota(jnp.int32, (span, head_width), 1) // HDD
    seen = jnp.broadcast_to(seen[None], (heads, span, span)).reshape(heads * span, span)
    for tile in range(frames // TF):
        rows = slice(tile * span, tile * span + span)
        queries, keys, values = (qkv_s[i, rows] for i in range(3))
        queries = jnp.concatenate(
            [jnp.where(head == h, queries, jnp.zeros_like(queries)) for h in range(heads)]
        )
        scores = lax.dot_general(queries, keys, NT, preferred_element_type=F32)
        weights = softmax_rounded(jnp.where(seen, scores * HDD**-0.5, -1e30))
        context = jnp.dot(weights, values, preferred_element_type=F32)
        picked = context[:span]
        for h in range(1, heads):
            picked = jnp.where(head == h, context[h * span : (h + 1) * span], picked)
        ctx_s[rows] = picked.astype(BF)
    mixed = u_s[...] + jnp.dot(ctx_s[...], dout[...], preferred_element_type=F32)
    logits = jnp.dot(rms(mixed), logit[...], preferred_element_type=F32)
    top = jnp.max(logits, axis=-1, keepdims=True)
    total = jnp.sum(jnp.exp(logits - top), axis=-1, keepdims=True)
    entry = lax.broadcasted_iota(jnp.int32, logits.shape, 1)
    picked = jnp.sum(jnp.where(entry == target[...], logits, 0.0), axis=-1, keepdims=True)
    o_ref[...] = jnp.log(total) + top - picked


def depth(x, parts, proj, dqkv, dout, logit, emb, target):
    count, width = emb.shape
    head_width = dout.shape[0]
    return pl.pallas_call(
        depth_kernel,
        out_shape=jax.ShapeDtypeStruct((count, 1), F32),
        in_specs=[vmem()] * 10,
        out_specs=vmem(),
        scratch_shapes=[
            pltpu.VMEM((count, width), F32),
            pltpu.VMEM((3, count, head_width), BF),
            pltpu.VMEM((count, head_width), BF),
        ],
        compiler_params=pltpu.CompilerParams(vmem_limit_bytes=16 * 2**20),
        cost_estimate=pl.CostEstimate(
            flops=2 * count * width * 5120, bytes_accessed=2**22, transcendentals=0
        ),
        name="depth",
    )(x, *parts, proj, dqkv, dout, logit, emb, target)


def rope_tables(rows):
    half = HD // 2
    frequency = 10000.0 ** (-jnp.arange(half, dtype=F32) / half)
    angles = jnp.arange(rows).astype(F32)[:, None] * frequency[None, :]
    cosine, sine = jnp.cos(angles), jnp.sin(angles)
    return (
        jnp.concatenate([cosine, cosine], axis=1),
        jnp.concatenate([-sine, sine], axis=1),
    )


def packed_qkv(qkv_weight):
    w = jnp.transpose(qkv_weight[0], (1, 0, 2))
    halves = []
    for i in range(2):
        cuts = [slice(512 * i + 256 * j, 512 * i + 256 * j + 256) for j in range(2)]
        halves.append(jnp.concatenate([w[k][:, cut] for cut in cuts for k in range(3)], axis=1))
    return jnp.stack(halves)


def packed_out(out_weight):
    o = out_weight[0]
    return jnp.stack([o[512 * i : 512 * i + 512].T for i in range(2)])


def local(
    frames_in, qkv_weight, out_weight, proj_weight, depth_qkv, depth_out, code_table,
    logit_weight, given_codes, given_delays,
):
    s = lax.axis_index("segment")
    f = lax.axis_index("frame")
    d = lax.axis_index("dp")
    row_count = frames_in.shape[1]
    part = row_count // 2
    streams = given_codes.shape[2]
    me = s * 2 + f

    def rows_of(i):
        i = i % SIDE
        return (i % 2) * row_count + (i // 2) * part

    sign = 1 - 2 * (d % 2)

    def place_of(starts):
        starts = (list(starts) + [0] * SIDE)[:SIDE]
        targets = [rows_of(me + k * sign + 4) for k in (0, 1, -1, 2)]
        return jnp.stack([*starts, *targets]).astype(jnp.int32)

    kept, got = [], []
    for packed in (packed_qkv(qkv_weight), packed_out(out_weight)):
        kept.append(lax.dynamic_index_in_dim(packed, s, 0, keepdims=False))
        given = lax.dynamic_index_in_dim(packed, 1 - s, 0, keepdims=False)
        got.append(xswap(given, [(0, 3), (3, 0), (1, 2), (2, 1)]))
    kept, got = (jnp.concatenate(parts, axis=1) for parts in (kept, got))
    first = jnp.where(s == 0, kept, got)
    w0 = lax.all_gather(first, "dp")
    frames = frames_in[0]
    normed = norm_rows(frames)
    far = xhop(tied(normed, got), 1)

    given_tail = lax.ppermute(given_codes[0, row_count - DMAX :], "frame", [(0, 1)])

    def prepare(after):
        codes, delays = tied((given_codes, given_delays), after)
        tail = tied(given_tail, after)
        extended = jnp.concatenate([tail, codes[0]], axis=0)
        extended = lax.dynamic_slice_in_dim(extended, s * part, part + DMAX, 0)
        targets = extended[DMAX : DMAX + part]
        for lag in range(1, DMAX + 1):
            targets = jnp.where(
                delays[None, :] == lag, extended[DMAX - lag : DMAX - lag + part], targets
            )
        frame = rows_of(me) + jnp.arange(part, dtype=jnp.int32)
        is_valid = frame[:, None] >= delays[None, :]
        targets = jnp.clip(targets, 0, code_table.shape[0] - 1)

        def tiled(a):
            return jnp.transpose(a.reshape(part // TF, TF, streams), (0, 2, 1)).reshape(-1)

        def behind(a):
            return jnp.concatenate([jnp.zeros_like(a[:, :1]), a[:, :-1]], axis=1)

        emb = jnp.take(code_table, tiled(behind(targets)), axis=0, mode="clip")
        emb = jnp.where(tiled(behind(is_valid))[:, None], emb, jnp.zeros_like(emb))
        return emb, tiled(targets)[:, None], is_valid, rope_tables(2 * row_count)

    emb, target, is_valid, tables = prepare(far)
    far, emb, target, tables, (kept, got) = lax.optimization_barrier(
        (far, emb, target, tables, (kept, got))
    )
    w1 = lax.all_gather(jnp.where(s == 0, got, kept), "dp")
    place0 = place_of([f * row_count, (1 - f) * row_count])
    sent = layer(place0, tables, [normed, far], w0)

    def spread(block):
        return [block, xhop(block, 1), xhop(block, -1), xhop2(block)]

    def scattered(sent):
        relayed, back = xhop(sent[3], 1), xhop(sent[2], -1)
        relayed = (sent[1].astype(F32) + relayed.astype(F32)).astype(BF)
        return [sent[0], xhop(relayed, 1), back]

    mine = lax.dynamic_slice_in_dim(frames, s * part, part, 0)
    x1, n1 = merge_rows(mine, scattered(sent))
    starts = [rows_of(me + k * sign + 4) for k in (0, -1, 1, 2)]
    sent = layer(place_of(starts), tables, spread(n1), w1)

    ready = [proj_weight, jnp.transpose(depth_qkv, (1, 0, 2)), depth_out, logit_weight]
    ready = load(tied(ready, sent))
    losses = depth(x1, scattered(sent), *ready, emb, target)
    losses = jnp.transpose(losses.reshape(part // TF, streams, TF), (0, 2, 1))
    losses = jnp.where(is_valid, losses.reshape(part, streams), 0.0)
    other = xhop2(losses)
    both = jnp.where(s == 0, jnp.stack([losses, other]), jnp.stack([other, losses]))
    return both.reshape(1, row_count, streams)


def solution(mesh):
    return jax.shard_map(
        local,
        mesh=mesh,
        in_specs=(
            P("dp", "frame", None),
            P("segment", "dp", None, "frame"),
            P("segment", "frame", "dp"),
            P(),
            P(),
            P(),
            P(),
            P(),
            P("dp", "frame", None),
            P(),
        ),
        out_specs=P("dp", "frame", None),
        check_vma=False,
    )
```
